32 devices in a mesh: batch: 16 (over z, y, x), seq: 2 (over core).
Axes of the slice: x: 2, y: 2, z: 4, core: 2. Of those that a mesh axis runs over, the one named last changes fastest.
Arguments:
- tokens: bfloat16 [16, 1024, 1024], P('batch', 'seq'), may hold values from -6 to 6
- cotangent: bfloat16 [16, 1024, 1024], P('batch', 'seq'), may hold values from -6 to 6
- w_in: float32 [1024, 3072], P(('batch', 'seq')), may hold values from -0.1875 to 0.1875
- first_in: float32 [1024, 3072], P(('batch', 'seq')), may hold values from -96 to 96
- second_in: float32 [1024, 3072], P(('batch', 'seq')), may hold values from 1146.88 to 7045.12
- conv_taps: float32 [1024, 3], P(('batch', 'seq')), may hold values from -3.5 to 3.5
- first_conv: float32 [1024, 3], P(('batch', 'seq')), may hold values from -96 to 96
- second_conv: float32 [1024, 3], P(('batch', 'seq')), may hold values from 1146.88 to 7045.12
- w_out: float32 [1024, 1024], P(('batch', 'seq')), may hold values from -0.1875 to 0.1875
- first_out: float32 [1024, 1024], P(('batch', 'seq')), may hold values from -96 to 96
- second_out: float32 [1024, 1024], P(('batch', 'seq')), may hold values from 1146.88 to 7045.12
- w_mlp: float32 [1024, 9216], P(('batch', 'seq')), may hold values from -0.1875 to 0.1875
- first_mlp: float32 [1024, 9216], P(('batch', 'seq')), may hold values from -24 to 24
- second_mlp: float32 [1024, 9216], P(('batch', 'seq')), may hold values from 73.728 to 442.368
- w_down: float32 [4608, 1024], P(('batch', 'seq')), may hold values from -0.09375 to 0.09375
- first_down: float32 [4608, 1024], P(('batch', 'seq')), may hold values from -48 to 48
- second_down: float32 [4608, 1024], P(('batch', 'seq')), may hold values from 294.912 to 1802.24
- norm_gains: float32 [1024, 2], P(('batch', 'seq')), may hold values from 0.5 to 1.5
- first_gains: float32 [1024, 2], P(('batch', 'seq')), may hold values from -160 to 160
- second_gains: float32 [1024, 2], P(('batch', 'seq')), may hold values from 3276.8 to 19660.8
Outputs:
- output: bfloat16 [16, 1024, 1024], P('batch', 'seq')
- grad_tokens: bfloat16 [16, 1024, 1024], P('batch', 'seq')
- first_in_next: float32 [1024, 3072], P(('batch', 'seq'))
- second_in_next: float32 [1024, 3072], P(('batch', 'seq'))
- w_in_next: float32 [1024, 3072], P(('batch', 'seq'))
- first_conv_next: float32 [1024, 3], P(('batch', 'seq'))
- second_conv_next: float32 [1024, 3], P(('batch', 'seq'))
- conv_taps_next: float32 [1024, 3], P(('batch', 'seq'))
- first_out_next: float32 [1024, 1024], P(('batch', 'seq'))
- second_out_next: float32 [1024, 1024], P(('batch', 'seq'))
- w_out_next: float32 [1024, 1024], P(('batch', 'seq'))
- first_mlp_next: float32 [1024, 9216], P(('batch', 'seq'))
- second_mlp_next: float32 [1024, 9216], P(('batch', 'seq'))
- w_mlp_next: float32 [1024, 9216], P(('batch', 'seq'))
- first_down_next: float32 [4608, 1024], P(('batch', 'seq'))
- second_down_next: float32 [4608, 1024], P(('batch', 'seq'))
- w_down_next: float32 [4608, 1024], P(('batch', 'seq'))
- first_gains_next: float32 [1024, 2], P(('batch', 'seq'))
- second_gains_next: float32 [1024, 2], P(('batch', 'seq'))
- norm_gains_next: float32 [1024, 2], P(('batch', 'seq'))
The draws below stay inside these ranges and needn't reach their ends.
All inputs are finite; a program needn't handle non-finite values.
Results may differ from the reference program's by a relative error of at most 0.012.
The reference program's roundings to bfloat16 on the way count: a program that leaves them out, or rounds other values in their place, can miss the bound.
Values may be sent and summed in bfloat16 or wider, within the bound.
A program may use at most 256 MiB of HBM per device.

```python
import math
import jax
import jax.numpy as jnp
from jax import lax

D = 1024
FF = 4608
LENGTH = 1024
STEP = 10
SEQS = 16
TOKENS = 16384


def steps_of(stream_key, dims, split, least, high):
    loudness, own = 1.0, jax.random.fold_in(stream_key, 6)
    for dim, parts in split:
        heights = jnp.exp(jax.random.uniform(jax.random.fold_in(own, dim), (parts,), jnp.float32, least / len(split), high / len(split)))
        loudness = loudness * jnp.repeat(heights, dims[dim] // parts).reshape([-1 if axis == dim else 1 for axis in range(len(dims))])
    return loudness


def bell_draw(own_key, shape, scale, limit, split=(), dtype=jnp.bfloat16):
    values = jax.random.normal(own_key, shape, jnp.float32) * scale
    if len(split) > 0:
        values = steps_of(own_key, shape, split, -0.22, 0.18) * values
    return jnp.clip(values, min=-limit, max=limit).astype(dtype)


def setup_inputs(seed: int = 0) -> dict:
    seeds = jax.random.split(jax.random.key(seed), 21)
    tokens = bell_draw(seeds[0], (SEQS, LENGTH, D), 1.0, 6.0, ((0, 16), (1, 2)))
    cotangent = bell_draw(seeds[1], (SEQS, LENGTH, D), 1.0, 6.0, ((0, 16), (1, 2)))
    w_in = bell_draw(seeds[2], (D, 3 * D), D ** -0.5, 0.1875, ((0, 32),), jnp.float32)
    first_in = bell_draw(seeds[3], (D, 3 * D), (0.13 * TOKENS ** 0.5), 96.0, ((0, 32),), jnp.float32)
    second_in = jnp.clip(jnp.exp(math.log(7045.12) - 1.81529 * jax.random.uniform(seeds[4], (D, 3 * D), jnp.float32) ** steps_of(seeds[4], (D, 3 * D), ((0, 32),), -0.2, 0.2)), 1146.88, 7045.12)
    conv_taps = bell_draw(seeds[5], (D, 3), 3 ** -0.5, 3.5, ((0, 32),), jnp.float32)
    first_conv = bell_draw(seeds[6], (D, 3), (0.13 * TOKENS ** 0.5), 96.0, ((0, 32),), jnp.float32)
    second_conv = jnp.clip(jnp.exp(math.log(7045.12) - 1.81529 * jax.random.uniform(seeds[7], (D, 3), jnp.float32) ** steps_of(seeds[7], (D, 3), ((0, 32),), -0.2, 0.2)), 1146.88, 7045.12)
    w_out = bell_draw(seeds[8], (D, D), D ** -0.5, 0.1875, ((0, 32),), jnp.float32)
    first_out = bell_draw(seeds[9], (D, D), (0.13 * TOKENS ** 0.5), 96.0, ((0, 32),), jnp.float32)
    second_out = jnp.clip(jnp.exp(math.log(7045.12) - 1.81529 * jax.random.uniform(seeds[10], (D, D), jnp.float32) ** steps_of(seeds[10], (D, D), ((0, 32),), -0.2, 0.2)), 1146.88, 7045.12)
    w_mlp = bell_draw(seeds[11], (D, 2 * FF), D ** -0.5, 0.1875, ((0, 32),), jnp.float32)
    first_mlp = bell_draw(seeds[12], (D, 2 * FF), (0.033 * TOKENS ** 0.5), 24.0, ((0, 32),), jnp.float32)
    second_mlp = jnp.clip(jnp.exp(math.log(442.368) - 1.7917595 * jax.random.uniform(seeds[13], (D, 2 * FF), jnp.float32) ** steps_of(seeds[13], (D, 2 * FF), ((0, 32),), -0.2, 0.2)), 73.728, 442.368)
    w_down = bell_draw(seeds[14], (FF, D), FF ** -0.5, 0.09375, ((0, 32),), jnp.float32)
    first_down = bell_draw(seeds[15], (FF, D), (0.066 * TOKENS ** 0.5), 48.0, ((0, 32),), jnp.float32)
    second_down = jnp.clip(jnp.exp(math.log(1802.24) - 1.81010865 * jax.random.uniform(seeds[16], (FF, D), jnp.float32) ** steps_of(seeds[16], (FF, D), ((0, 32),), -0.2, 0.2)), 294.912, 1802.24)
    norm_gains = jnp.clip(1.0 + 0.1 * jax.random.normal(seeds[17], (D, 2), jnp.float32), 0.5, 1.5)
    first_gains = bell_draw(seeds[18], (D, 2), (0.22 * TOKENS ** 0.5), 160.0, ((0, 32),), jnp.float32)
    second_gains = jnp.clip(jnp.exp(math.log(19660.8) - 1.7917595 * jax.random.uniform(seeds[19], (D, 2), jnp.float32) ** steps_of(seeds[19], (D, 2), ((0, 32),), -0.2, 0.2)), 3276.8, 19660.8)
    return dict(tokens=tokens, cotangent=cotangent, w_in=w_in, first_in=first_in, second_in=second_in, conv_taps=conv_taps, first_conv=first_conv, second_conv=second_conv, w_out=w_out, first_out=first_out, second_out=second_out, w_mlp=w_mlp, first_mlp=first_mlp, second_mlp=second_mlp, w_down=w_down, first_down=first_down, second_down=second_down, norm_gains=norm_gains, first_gains=first_gains, second_gains=second_gains)


EPS = 1e-05
BETA_ONE = 0.9
BETA_TWO = 0.95
ADAM_EPS = 1e-08
DECAY = 0.1
HIGHEST = lax.Precision.HIGHEST

@jax.custom_vjp
def low(v):
    return lax.optimization_barrier(v.astype(jnp.bfloat16)).astype(jnp.float32)

@jax.custom_vjp
def low_back(v):
    return v

def low_keep(v):
    return (low(v), None)

def low_pass(kept, grad):
    return (grad,)

def back_keep(v):
    return (v, None)

def back_low(kept, grad):
    return (low(grad),)
low.defvjp(low_keep, low_pass)
low_back.defvjp(back_keep, back_low)

def rms_scale(values):
    return lax.rsqrt(lax.optimization_barrier(jnp.mean(values * values, axis=-1, keepdims=True)) + EPS)

def forward(w_in, conv_taps, w_out, w_mlp, w_down, norm_gains, inputs):
    w_in = low(w_in)
    conv_taps = low(conv_taps)
    w_out = low(w_out)
    w_mlp = low(w_mlp)
    w_down = low(w_down)
    norm_gains = low(norm_gains)
    normed = low(inputs * rms_scale(inputs) * norm_gains[:, 0])
    projected = low_back(jnp.einsum('gld,de->gle', normed, w_in, precision=HIGHEST))
    b_gate = projected[..., :D]
    c_gate = projected[..., D:2 * D]
    values = projected[..., 2 * D:]
    gated_rows = low(b_gate * values)
    padded = jnp.pad(gated_rows, ((0, 0), (2, 0), (0, 0)))
    conv_out = low_back(padded[:, :-2] * conv_taps[:, 0] + padded[:, 1:-1] * conv_taps[:, 1] + padded[:, 2:] * conv_taps[:, 2])
    mixed_rows = low(c_gate * conv_out)
    branch = low_back(jnp.einsum('gld,de->gle', mixed_rows, w_out, precision=HIGHEST))
    middle = inputs + branch
    normed_two = low(middle * rms_scale(middle) * norm_gains[:, 1])
    gate_up = low_back(jnp.einsum('gld,de->gle', normed_two, w_mlp, precision=HIGHEST))
    hidden = low(jax.nn.silu(gate_up[..., :FF]) * gate_up[..., FF:])
    return middle + jnp.einsum('glf,fd->gld', hidden, w_down, precision=HIGHEST)

def adamw(weight, gradient, first_moment, second_moment, learn_rate):
    new_first = BETA_ONE * first_moment + (1.0 - BETA_ONE) * gradient
    new_second = BETA_TWO * second_moment + (1.0 - BETA_TWO) * gradient * gradient
    first_hat = new_first / (1.0 - BETA_ONE ** STEP)
    second_hat = new_second / (1.0 - BETA_TWO ** STEP)
    new_weight = weight - learn_rate * (first_hat / (jnp.sqrt(second_hat) + ADAM_EPS) + DECAY * weight)
    return (new_first, new_second, new_weight)

def reference(tokens, cotangent, w_in, first_in, second_in, conv_taps, first_conv, second_conv, w_out, first_out, second_out, w_mlp, first_mlp, second_mlp, w_down, first_down, second_down, norm_gains, first_gains, second_gains):
    params = (w_in, conv_taps, w_out, w_mlp, w_down, norm_gains)
    group_seqs = 1
    for option in (2, 4):
        if SEQS % option == 0 and option * LENGTH <= 4096:
            group_seqs = option
    block_count = SEQS // group_seqs
    token_blocks = tokens.reshape(block_count, group_seqs, LENGTH, D)
    back_blocks = cotangent.reshape(block_count, group_seqs, LENGTH, D)

    def block_step(totals, block_pair):
        inputs = block_pair[0].astype(jnp.float32)
        incoming = block_pair[1].astype(jnp.float32)
        result, pull = jax.vjp(forward, w_in, conv_taps, w_out, w_mlp, w_down, norm_gains, inputs)
        gradients = pull(incoming)
        totals = tuple((total + grad_part for total, grad_part in zip(totals, gradients[:6])))
        return (totals, (result.astype(jnp.bfloat16), gradients[6].astype(jnp.bfloat16)))
    zero_grads = tuple((jnp.zeros(param.shape, jnp.float32) for param in params))
    totals, (result_blocks, input_grads) = lax.scan(block_step, zero_grads, (token_blocks, back_blocks))
    output = result_blocks.reshape(SEQS, LENGTH, D)
    grad_tokens = input_grads.reshape(SEQS, LENGTH, D)
    rate_wide = 2.0 / D ** 0.5
    rate_down = 2.0 / FF ** 0.5
    in_new = adamw(w_in, totals[0], first_in, second_in, rate_wide)
    conv_new = adamw(conv_taps, totals[1], first_conv, second_conv, 1.0)
    out_new = adamw(w_out, totals[2], first_out, second_out, rate_wide)
    mlp_new = adamw(w_mlp, totals[3], first_mlp, second_mlp, rate_wide)
    down_new = adamw(w_down, totals[4], first_down, second_down, rate_down)
    gains_new = adamw(norm_gains, totals[5], first_gains, second_gains, 0.6)
    return (output, grad_tokens, in_new[0], in_new[1], in_new[2], conv_new[0], conv_new[1], conv_new[2], out_new[0], out_new[1], out_new[2], mlp_new[0], mlp_new[1], mlp_new[2], down_new[0], down_new[1], down_new[2], gains_new[0], gains_new[1], gains_new[2])
```

```python
import jax
import jax.numpy as jnp
from jax import lax
from jax.sharding import PartitionSpec as P

D = 1024
FF = 4608
STEP = 10
SMALL = 128


EPS = 1e-05
BETA_ONE = 0.9
BETA_TWO = 0.95
ADAM_EPS = 1e-08
DECAY = 0.1


def from_behind(block, axis, distance):
    devices = range(lax.axis_size(axis))
    route = [(i - distance, i) for i in devices if i - distance in devices]
    return lax.ppermute(block, axis, route)


def rms_scale(values):
    return lax.rsqrt(jnp.mean(values * values, axis=-1, keepdims=True) + EPS)


def norm_back(values, inv_scale, gain_row, grad_normed):
    weighted = grad_normed * gain_row
    gain_grad = jnp.sum(grad_normed * values * inv_scale, axis=(0, 1))
    projection = jnp.mean(weighted * values, axis=-1, keepdims=True)
    grad_values = inv_scale * weighted - values * (inv_scale * inv_scale * inv_scale) * projection
    return (grad_values, gain_grad)


def adamw(weight, gradient, first_moment, second_moment, learn_rate):
    new_first = BETA_ONE * first_moment + (1.0 - BETA_ONE) * gradient
    new_second = BETA_TWO * second_moment + (1.0 - BETA_TWO) * gradient * gradient
    first_hat = new_first / (1.0 - BETA_ONE**STEP)
    second_hat = new_second / (1.0 - BETA_TWO**STEP)
    new_weight = weight - learn_rate * (
        first_hat / (jnp.sqrt(second_hat) + ADAM_EPS) + DECAY * weight
    )
    return (new_first, new_second, new_weight)


def shards(
    tokens,
    cotangent,
    w_in,
    first_in,
    second_in,
    conv_taps,
    first_conv,
    second_conv,
    w_out,
    first_out,
    second_out,
    w_mlp,
    first_mlp,
    second_mlp,
    w_down,
    first_down,
    second_down,
    norm_gains,
    first_gains,
    second_gains,
):
    half_type = jnp.bfloat16
    rows = w_in.shape[0]
    both = ("batch", "seq")
    spare = jnp.zeros((rows, SMALL - 5), half_type)
    first_pack = jnp.concatenate(
        [
            w_in.astype(half_type),
            w_out.astype(half_type),
            conv_taps.astype(half_type),
            norm_gains.astype(half_type),
            spare,
        ],
        axis=1,
    )
    first_low = lax.all_gather(first_pack, both, axis=0, tiled=True)
    mlp_low = lax.all_gather(w_mlp.astype(half_type), both, axis=0, tiled=True)
    down_low = lax.all_gather(w_down.astype(half_type), both, axis=0, tiled=True)
    in_low = first_low[:, : 3 * D]
    out_low = first_low[:, 3 * D : 4 * D]
    conv_low = first_low[:, 4 * D : 4 * D + 3]
    gain_low = first_low[:, 4 * D + 3 : 4 * D + 5]
    tap_values = conv_low.astype(jnp.float32)
    gain_one = gain_low[:, 0].astype(jnp.float32)
    gain_two = gain_low[:, 1].astype(jnp.float32)
    inputs = tokens.astype(jnp.float32)
    scale_one = rms_scale(inputs)
    normed = (inputs * scale_one * gain_one).astype(half_type)
    projected = jnp.einsum("spd,de->spe", normed, in_low, preferred_element_type=jnp.float32)
    b_gate = projected[..., :D]
    c_gate = projected[..., D : 2 * D]
    values = projected[..., 2 * D :]
    gated_rows = (b_gate * values).astype(half_type)
    length = gated_rows.shape[1]
    earlier = from_behind(gated_rows[:, length - 2 :], "seq", 1)
    padded = jnp.concatenate([earlier, gated_rows], axis=1).astype(jnp.float32)
    conv_out = (
        padded[:, :length] * tap_values[:, 0]
        + padded[:, 1 : length + 1] * tap_values[:, 1]
        + padded[:, 2:] * tap_values[:, 2]
    )
    mixed_rows = (c_gate * conv_out).astype(half_type)
    branch = jnp.einsum("spd,de->spe", mixed_rows, out_low, preferred_element_type=jnp.float32)
    middle = inputs + branch
    scale_two = rms_scale(middle)
    normed_two = (middle * scale_two * gain_two).astype(half_type)
    gate_up = jnp.einsum("spd,de->spe", normed_two, mlp_low, preferred_element_type=jnp.float32)
    gate_part = gate_up[..., :FF]
    upward = gate_up[..., FF:]
    hidden = (jax.nn.silu(gate_part) * upward).astype(half_type)
    output = (
        middle + jnp.einsum("spf,fd->spd", hidden, down_low, preferred_element_type=jnp.float32)
    ).astype(half_type)
    grad_hidden = jnp.einsum("spd,fd->spf", cotangent, down_low, preferred_element_type=jnp.float32)
    sigmoid_gate = jax.nn.sigmoid(gate_part)
    grad_gate = grad_hidden * upward * (sigmoid_gate * (1.0 + gate_part * (1.0 - sigmoid_gate)))
    grad_upward = grad_hidden * (gate_part * sigmoid_gate)
    grad_gate_up = jnp.concatenate([grad_gate, grad_upward], axis=-1).astype(half_type)
    grad_normed_two = jnp.einsum(
        "spe,de->spd", grad_gate_up, mlp_low, preferred_element_type=jnp.float32
    )
    grad_middle, gain_grad_two = norm_back(middle, scale_two, gain_two, grad_normed_two)
    grad_middle = cotangent.astype(jnp.float32) + grad_middle
    grad_branch = grad_middle.astype(half_type)
    grad_mixed = jnp.einsum("spe,de->spd", grad_branch, out_low, preferred_element_type=jnp.float32)
    grad_cgate = grad_mixed * conv_out
    grad_conv = (grad_mixed * c_gate).astype(half_type)
    later = from_behind(grad_conv[:, :2], "seq", -1)
    extended = jnp.concatenate([grad_conv, later], axis=1).astype(jnp.float32)
    grad_taps = jnp.stack(
        [
            jnp.sum(extended[:, :length] * padded[:, offset : offset + length], axis=(0, 1))
            for offset in range(3)
        ],
        axis=-1,
    )
    grad_gated = (
        extended[:, :length] * tap_values[:, 2]
        + extended[:, 1 : length + 1] * tap_values[:, 1]
        + extended[:, 2:] * tap_values[:, 0]
    )
    grad_proj = jnp.concatenate(
        [grad_gated * values, grad_cgate, grad_gated * b_gate], axis=-1
    ).astype(half_type)
    grad_normed = jnp.einsum("spe,de->spd", grad_proj, in_low, preferred_element_type=jnp.float32)
    grad_inputs, gain_grad_one = norm_back(inputs, scale_one, gain_one, grad_normed)
    grad_tokens = (grad_middle + grad_inputs).astype(half_type)
    part_down = jnp.einsum("spf,spd->fd", hidden, cotangent, preferred_element_type=jnp.float32)
    part_mlp = jnp.einsum(
        "spd,spe->de", normed_two, grad_gate_up, preferred_element_type=jnp.float32
    )
    part_out = jnp.einsum(
        "spd,spe->de", mixed_rows, grad_branch, preferred_element_type=jnp.float32
    )
    part_in = jnp.einsum("spd,spe->de", normed, grad_proj, preferred_element_type=jnp.float32)
    small_grads = jnp.concatenate(
        [
            grad_taps,
            jnp.stack([gain_grad_one, gain_grad_two], axis=-1),
            jnp.zeros((D, SMALL - 5), jnp.float32),
        ],
        axis=-1,
    )
    last_pack = jnp.concatenate(
        [part_in.astype(half_type), part_out.astype(half_type), small_grads.astype(half_type)],
        axis=1,
    )
    grad_down = lax.psum_scatter(
        part_down.astype(half_type), both, scatter_dimension=0, tiled=True
    ).astype(jnp.float32)
    grad_mlp = lax.psum_scatter(
        part_mlp.astype(half_type), both, scatter_dimension=0, tiled=True
    ).astype(jnp.float32)
    last_sum = lax.psum_scatter(last_pack, both, scatter_dimension=0, tiled=True).astype(
        jnp.float32
    )
    grad_inw = last_sum[:, : 3 * D]
    grad_outw = last_sum[:, 3 * D : 4 * D]
    grad_tapw = last_sum[:, 4 * D : 4 * D + 3]
    grad_gains = last_sum[:, 4 * D + 3 : 4 * D + 5]
    rate_wide = 2.0 / D**0.5
    rate_down = 2.0 / FF**0.5
    in_new = adamw(w_in, grad_inw, first_in, second_in, rate_wide)
    conv_new = adamw(conv_taps, grad_tapw, first_conv, second_conv, 1.0)
    out_new = adamw(w_out, grad_outw, first_out, second_out, rate_wide)
    mlp_new = adamw(w_mlp, grad_mlp, first_mlp, second_mlp, rate_wide)
    down_new = adamw(w_down, grad_down, first_down, second_down, rate_down)
    gains_new = adamw(norm_gains, grad_gains, first_gains, second_gains, 0.6)
    return (
        output,
        grad_tokens,
        in_new[0],
        in_new[1],
        in_new[2],
        conv_new[0],
        conv_new[1],
        conv_new[2],
        out_new[0],
        out_new[1],
        out_new[2],
        mlp_new[0],
        mlp_new[1],
        mlp_new[2],
        down_new[0],
        down_new[1],
        down_new[2],
        gains_new[0],
        gains_new[1],
        gains_new[2],
    )


def solution(mesh):
    placed = (
        P("batch", "seq", None),
        P("batch", "seq", None),
        P(("batch", "seq"), None),
        P(("batch", "seq"), None),
        P(("batch", "seq"), None),
        P(("batch", "seq"), None),
        P(("batch", "seq"), None),
        P(("batch", "seq"), None),
        P(("batch", "seq"), None),
        P(("batch", "seq"), None),
        P(("batch", "seq"), None),
        P(("batch", "seq"), None),
        P(("batch", "seq"), None),
        P(("batch", "seq"), None),
        P(("batch", "seq"), None),
        P(("batch", "seq"), None),
        P(("batch", "seq"), None),
        P(("batch", "seq"), None),
        P(("batch", "seq"), None),
        P(("batch", "seq"), None),
    )
    return jax.shard_map(
        shards,
        mesh=mesh,
        in_specs=placed,
        out_specs=(
            P("batch", "seq", None),
            P("batch", "seq", None),
            P(("batch", "seq"), None),
            P(("batch", "seq"), None),
            P(("batch", "seq"), None),
            P(("batch", "seq"), None),
            P(("batch", "seq"), None),
            P(("batch", "seq"), None),
            P(("batch", "seq"), None),
            P(("batch", "seq"), None),
            P(("batch", "seq"), None),
            P(("batch", "seq"), None),
            P(("batch", "seq"), None),
            P(("batch", "seq"), None),
            P(("batch", "seq"), None),
            P(("batch", "seq"), None),
            P(("batch", "seq"), None),
            P(("batch", "seq"), None),
            P(("batch", "seq"), None),
            P(("batch", "seq"), None),
        ),
        check_vma=False,
    )
```

```python
import jax
import jax.numpy as jnp
from jax import lax
from jax.sharding import PartitionSpec as P

D = 1024
FF = 4608
STEP = 10
SMALL = 128


EPS = 1e-05
BETA_ONE = 0.9
BETA_TWO = 0.95
ADAM_EPS = 1e-08
DECAY = 0.1


def from_behind(block, axis, distance):
    devices = range(lax.axis_size(axis))
    route = [(i - distance, i) for i in devices if i - distance in devices]
    return lax.ppermute(block, axis, route)


def paired():
    return lax.axis_size("seq") == 2 and D % (32 * lax.axis_size("batch")) == 0


def core_sum(part):
    if not paired():
        return part
    me = lax.axis_index("seq")
    blocks = part.reshape(lax.axis_size("batch"), 2, -1, part.shape[1])
    theirs = lax.dynamic_index_in_dim(blocks, 1 - me, axis=1, keepdims=False)
    mine = lax.dynamic_index_in_dim(blocks, me, axis=1, keepdims=False)
    arrived = lax.ppermute(theirs, "seq", [(0, 1), (1, 0)])
    total = mine.astype(jnp.float32) + arrived.astype(jnp.float32)
    return total.astype(part.dtype).reshape(-1, part.shape[1])


def spread_sum(half):
    axes = "batch" if paired() else ("batch", "seq")
    return lax.psum_scatter(half, axes, scatter_dimension=0, tiled=True)


def rms_scale(values):
    return lax.rsqrt(jnp.mean(values * values, axis=-1, keepdims=True) + EPS)


def norm_back(values, inv_scale, gain_row, grad_normed):
    weighted = grad_normed * gain_row
    gain_grad = jnp.sum(grad_normed * values * inv_scale, axis=(0, 1))
    projection = jnp.mean(weighted * values, axis=-1, keepdims=True)
    grad_values = inv_scale * weighted - values * (inv_scale * inv_scale * inv_scale) * projection
    return (grad_values, gain_grad)


def adamw(weight, gradient, first_moment, second_moment, learn_rate):
    new_first = BETA_ONE * first_moment + (1.0 - BETA_ONE) * gradient
    new_second = BETA_TWO * second_moment + (1.0 - BETA_TWO) * gradient * gradient
    first_hat = new_first / (1.0 - BETA_ONE**STEP)
    second_hat = new_second / (1.0 - BETA_TWO**STEP)
    new_weight = weight - learn_rate * (
        first_hat / (jnp.sqrt(second_hat) + ADAM_EPS) + DECAY * weight
    )
    return (new_first, new_second, new_weight)


def shards(
    tokens,
    cotangent,
    w_in,
    first_in,
    second_in,
    conv_taps,
    first_conv,
    second_conv,
    w_out,
    first_out,
    second_out,
    w_mlp,
    first_mlp,
    second_mlp,
    w_down,
    first_down,
    second_down,
    norm_gains,
    first_gains,
    second_gains,
):
    half_type = jnp.bfloat16
    rows = w_in.shape[0]
    both = ("batch", "seq")
    spare = jnp.zeros((rows, SMALL - 5), half_type)
    wide_pack = jnp.concatenate(
        [
            w_mlp.astype(half_type),
            w_in.astype(half_type),
            w_out.astype(half_type),
            conv_taps.astype(half_type),
            norm_gains.astype(half_type),
            spare,
        ],
        axis=1,
    )
    wide_low = lax.all_gather(wide_pack, both, axis=0, tiled=True)
    down_low = lax.all_gather(w_down.astype(half_type), both, axis=0, tiled=True)
    mlp_low = wide_low[:, : 2 * FF]
    in_low = wide_low[:, 2 * FF : 2 * FF + 3 * D]
    out_low = wide_low[:, 2 * FF + 3 * D : 2 * FF + 4 * D]
    conv_low = wide_low[:, 2 * FF + 4 * D : 2 * FF + 4 * D + 3]
    gain_low = wide_low[:, 2 * FF + 4 * D + 3 : 2 * FF + 4 * D + 5]
    tap_values = conv_low.astype(jnp.float32)
    gain_one = gain_low[:, 0].astype(jnp.float32)
    gain_two = gain_low[:, 1].astype(jnp.float32)
    inputs = tokens.astype(jnp.float32)
    scale_one = rms_scale(inputs)
    normed = (inputs * scale_one * gain_one).astype(half_type)
    projected = jnp.einsum("spd,de->spe", normed, in_low, preferred_element_type=jnp.float32)
    b_gate = projected[..., :D]
    c_gate = projected[..., D : 2 * D]
    values = projected[..., 2 * D :]
    gated_rows = (b_gate * values).astype(half_type)
    length = gated_rows.shape[1]
    earlier = from_behind(gated_rows[:, length - 2 :], "seq", 1)
    padded = jnp.concatenate([earlier, gated_rows], axis=1).astype(jnp.float32)
    conv_out = (
        padded[:, :length] * tap_values[:, 0]
        + padded[:, 1 : length + 1] * tap_values[:, 1]
        + padded[:, 2:] * tap_values[:, 2]
    )
    mixed_rows = (c_gate * conv_out).astype(half_type)
    branch = jnp.einsum("spd,de->spe", mixed_rows, out_low, preferred_element_type=jnp.float32)
    middle = inputs + branch
    scale_two = rms_scale(middle)
    normed_two = (middle * scale_two * gain_two).astype(half_type)
    gate_up = jnp.einsum("spd,de->spe", normed_two, mlp_low, preferred_element_type=jnp.float32)
    gate_part = gate_up[..., :FF]
    upward = gate_up[..., FF:]
    hidden = (jax.nn.silu(gate_part) * upward).astype(half_type)
    output = (
        middle + jnp.einsum("spf,fd->spd", hidden, down_low, preferred_element_type=jnp.float32)
    ).astype(half_type)
    grad_hidden = jnp.einsum("spd,fd->spf", cotangent, down_low, preferred_element_type=jnp.float32)
    sigmoid_gate = jax.nn.sigmoid(gate_part)
    grad_gate = grad_hidden * upward * (sigmoid_gate * (1.0 + gate_part * (1.0 - sigmoid_gate)))
    grad_upward = grad_hidden * (gate_part * sigmoid_gate)
    grad_gate_up = jnp.concatenate([grad_gate, grad_upward], axis=-1).astype(half_type)
    grad_normed_two = jnp.einsum(
        "spe,de->spd", grad_gate_up, mlp_low, preferred_element_type=jnp.float32
    )
    part_down = jnp.einsum("spf,spd->fd", hidden, cotangent, preferred_element_type=jnp.float32)
    down_half = core_sum(part_down.astype(half_type))
    down_half, grad_normed_two = lax.optimization_barrier((down_half, grad_normed_two))
    down_sum = spread_sum(down_half)
    grad_middle, gain_grad_two = norm_back(middle, scale_two, gain_two, grad_normed_two)
    grad_middle = cotangent.astype(jnp.float32) + grad_middle
    grad_branch = grad_middle.astype(half_type)
    grad_mixed = jnp.einsum("spe,de->spd", grad_branch, out_low, preferred_element_type=jnp.float32)
    grad_cgate = grad_mixed * conv_out
    grad_conv = (grad_mixed * c_gate).astype(half_type)
    later = from_behind(grad_conv[:, :2], "seq", -1)
    extended = jnp.concatenate([grad_conv, later], axis=1).astype(jnp.float32)
    grad_taps = jnp.stack(
        [
            jnp.sum(extended[:, :length] * padded[:, offset : offset + length], axis=(0, 1))
            for offset in range(3)
        ],
        axis=-1,
    )
    grad_gated = (
        extended[:, :length] * tap_values[:, 2]
        + extended[:, 1 : length + 1] * tap_values[:, 1]
        + extended[:, 2:] * tap_values[:, 0]
    )
    grad_proj = jnp.concatenate(
        [grad_gated * values, grad_cgate, grad_gated * b_gate], axis=-1
    ).astype(half_type)
    grad_normed = jnp.einsum("spe,de->spd", grad_proj, in_low, preferred_element_type=jnp.float32)
    grad_inputs, gain_grad_one = norm_back(inputs, scale_one, gain_one, grad_normed)
    grad_tokens = (grad_middle + grad_inputs).astype(half_type)
    part_mlp = jnp.einsum(
        "spd,spe->de", normed_two, grad_gate_up, preferred_element_type=jnp.float32
    )
    part_out = jnp.einsum(
        "spd,spe->de", mixed_rows, grad_branch, preferred_element_type=jnp.float32
    )
    part_in = jnp.einsum("spd,spe->de", normed, grad_proj, preferred_element_type=jnp.float32)
    small_grads = jnp.concatenate(
        [
            grad_taps,
            jnp.stack([gain_grad_one, gain_grad_two], axis=-1),
            jnp.zeros((D, SMALL - 5), jnp.float32),
        ],
        axis=-1,
    )
    wide_half = jnp.concatenate(
        [
            core_sum(part.astype(half_type))
            for part in (part_mlp, part_in, part_out, small_grads)
        ],
        axis=1,
    )
    wide_half, down_sum = lax.optimization_barrier((wide_half, down_sum))
    grad_down = down_sum.astype(jnp.float32)
    wide_sum = spread_sum(wide_half).astype(jnp.float32)
    grad_mlp = wide_sum[:, : 2 * FF]
    last_sum = wide_sum[:, 2 * FF :]
    grad_inw = last_sum[:, : 3 * D]
    grad_outw = last_sum[:, 3 * D : 4 * D]
    grad_tapw = last_sum[:, 4 * D : 4 * D + 3]
    grad_gains = last_sum[:, 4 * D + 3 : 4 * D + 5]
    rate_wide = 2.0 / D**0.5
    rate_down = 2.0 / FF**0.5
    in_new = adamw(w_in, grad_inw, first_in, second_in, rate_wide)
    conv_new = adamw(conv_taps, grad_tapw, first_conv, second_conv, 1.0)
    out_new = adamw(w_out, grad_outw, first_out, second_out, rate_wide)
    mlp_new = adamw(w_mlp, grad_mlp, first_mlp, second_mlp, rate_wide)
    down_new = adamw(w_down, grad_down, first_down, second_down, rate_down)
    gains_new = adamw(norm_gains, grad_gains, first_gains, second_gains, 0.6)
    return (
        output,
        grad_tokens,
        in_new[0],
        in_new[1],
        in_new[2],
        conv_new[0],
        conv_new[1],
        conv_new[2],
        out_new[0],
        out_new[1],
        out_new[2],
        mlp_new[0],
        mlp_new[1],
        mlp_new[2],
        down_new[0],
        down_new[1],
        down_new[2],
        gains_new[0],
        gains_new[1],
        gains_new[2],
    )


def solution(mesh):
    placed = (
        P("batch", "seq", None),
        P("batch", "seq", None),
        P(("batch", "seq"), None),
        P(("batch", "seq"), None),
        P(("batch", "seq"), None),
        P(("batch", "seq"), None),
        P(("batch", "seq"), None),
        P(("batch", "seq"), None),
        P(("batch", "seq"), None),
        P(("batch", "seq"), None),
        P(("batch", "seq"), None),
        P(("batch", "seq"), None),
        P(("batch", "seq"), None),
        P(("batch", "seq"), None),
        P(("batch", "seq"), None),
        P(("batch", "seq"), None),
        P(("batch", "seq"), None),
        P(("batch", "seq"), None),
        P(("batch", "seq"), None),
        P(("batch", "seq"), None),
    )
    return jax.shard_map(
        shards,
        mesh=mesh,
        in_specs=placed,
        out_specs=(
            P("batch", "seq", None),
            P("batch", "seq", None),
            P(("batch", "seq"), None),
            P(("batch", "seq"), None),
            P(("batch", "seq"), None),
            P(("batch", "seq"), None),
            P(("batch", "seq"), None),
            P(("batch", "seq"), None),
            P(("batch", "seq"), None),
            P(("batch", "seq"), None),
            P(("batch", "seq"), None),
            P(("batch", "seq"), None),
            P(("batch", "seq"), None),
            P(("batch", "seq"), None),
            P(("batch", "seq"), None),
            P(("batch", "seq"), None),
            P(("batch", "seq"), None),
            P(("batch", "seq"), None),
            P(("batch", "seq"), None),
            P(("batch", "seq"), None),
        ),
        check_vma=False,
    )
```
